32 devices in a mesh: seq: 8 (over y, x, core), head: 4 (over z).
Axes of the slice: x: 2, y: 2, z: 4, core: 2. Of those that a mesh axis runs over, the one named last changes fastest.
Arguments:
- attn_queries: float32 [2048, 4096], P('seq', 'head'), may hold values from -6 to 6
- attn_keys: float32 [2048, 4096], P('seq', 'head'), may hold values from -6 to 6
- attn_values: float32 [2048, 4096], P('seq', 'head'), may hold values from -6 to 6
- head_gain: float32 [128], replicated, may hold values from 0.25 to 1.75
- out_weight: bfloat16 [4096, 2048], P('head'), may hold values from -0.09375 to 0.09375
- residual_in: bfloat16 [2048, 2048], P(('seq', 'head')), may hold values from -6 to 6
- norm_gain: float32 [2048], replicated, may hold values from 0.25 to 1.75
- routed_experts: int32 [2048, 8], P(('seq', 'head')), may hold values from 0 to 31, all different within a row; in each aligned block of 64 rows (0 to 63, 64 to 127, ...) at most 40 rows name the same one
- gate_weights: float32 [2048, 8], P(('seq', 'head')), may hold values from 0.05 to 1
- expert_gate: bfloat16 [32, 2048, 768], P(('seq', 'head')), may hold values from -0.125 to 0.125
- expert_up: bfloat16 [32, 2048, 768], P(('seq', 'head')), may hold values from -0.125 to 0.125
- expert_down: bfloat16 [32, 768, 2048], P(('seq', 'head')), may hold values from -0.21875 to 0.21875
Outputs:
- attn_out: bfloat16 [2048, 2048], P(('seq', 'head'))
- moe_out: bfloat16 [2048, 2048], P(('seq', 'head'))
The draws below stay inside these ranges and needn't reach their ends.
Inputs may be any that keep to these rules, and one draw needn't show every extreme that they name: `routed_experts`: the 8 experts of a token differ. In each aligned block of 64 rows no expert is named by more than 40 rows, and in some block one expert is named by exactly 40 rows.
All inputs are finite; a program needn't handle non-finite values.
Results may differ from the reference program's by a relative error of at most 0.03.
Values may be sent and summed in bfloat16 or wider, within the bound.
A program may use at most 64 MiB of HBM per device.

```python
import math
import jax
import jax.numpy as jnp
import numpy as np
from jax import lax

D = 2048
HEADS = 32
HD = 128
FF = 768
TOPK = 8
TOKENS = 2048
ROWS_DEV = 64
EXPERTS = 32
CAP = 40


def block_levels(own_key, extent, shards, least, high):
    gain, own = 1.0, jax.random.fold_in(own_key, 6)
    for position, parts in shards:
        heights = jnp.exp(jax.random.uniform(jax.random.fold_in(own, position), (parts,), jnp.float32, least / len(shards), high / len(shards)))
        gain = gain * jnp.repeat(heights, extent[position] // parts).reshape([-1 if axis == position else 1 for axis in range(len(extent))])
    return gain


def deal_out(own_key, own, number, rows, number_of, top, limit, slope):
    sequence = jax.random.permutation(own_key, number_of)
    heavy_load, common = portions_of(number_of, rows * top, limit, slope, True), portions_of(number_of, rows * top, limit, slope, False)
    places = jnp.arange(number_of)

    def named(tallies, turn):
        used = int((tallies > 0).sum())
        fixed = max(1, used // 4)
        moved = fixed + (places - fixed + turn * (used - fixed)) % max(1, number_of - fixed)
        return jnp.zeros((number_of,), jnp.int32).at[sequence[jnp.where(places < fixed, places, moved)]].set(jnp.asarray(tallies, jnp.int32))

    tallies = jnp.where(number % 4 == 0, named(heavy_load, number // 4), named(common, number - number // 4 - 1))
    mixed = jax.random.permutation(jax.random.fold_in(own, 3), number_of)
    giver, sink = mixed[0:number_of // 2 * 2:2], mixed[1:number_of // 2 * 2:2]
    room = jnp.minimum(tallies[giver] - 1, limit - tallies[sink]) // 2
    room = jnp.where((giver == sequence[0]) | (sink == sequence[0]) | (tallies[sink] == 0), 0, jnp.maximum(room, 0))
    moved = jax.random.randint(jax.random.fold_in(own, 4), (number_of // 2,), 0, 1 << 20) % (room + 1)
    tallies = tallies.at[giver].add(-moved).at[sink].add(moved)
    items = jnp.searchsorted(jnp.cumsum(tallies), jnp.arange(rows * top), side="right").astype(jnp.int32)
    listing = items.reshape(top, rows).T
    listing = listing[jax.random.permutation(jax.random.fold_in(own, 1), rows)]
    turn = jax.random.randint(jax.random.fold_in(own, 2), (rows, 1), 0, top)
    return jnp.take_along_axis(listing, (jnp.arange(top)[None, :] + turn) % top, axis=1)


def portions_of(count, total, reach, slope, full):
    portions = [(1 << 20) // math.isqrt(rank ** slope) + 1 for rank in range(1, count + 1)]
    largest = reach if full else min(reach, max(-(-total // count), total * portions[0] // sum(portions)))
    least = 1 if total - largest >= count - 1 else 0
    given, spare = [largest] + [least] * (count - 1), total - largest - least * (count - 1)
    while spare > 0:
        candidates = [i for i in range(1, count) if given[i] < largest] or [i for i in range(1, count) if given[i] < reach]
        mass, left = sum([portions[i] for i in candidates]), spare
        for i in candidates:
            more = min(reach - given[i], max(1, left * portions[i] // mass), spare)
            given[i] = given[i] + more
            spare = spare - more
    return np.array(given)


def normal_values(key, dims, spread, bound, shards=(), held_as=jnp.bfloat16):
    level = block_levels(key, dims, shards, -0.22, 0.18) if shards else 1.0
    drawn = jax.random.normal(key, dims, jnp.float32) * spread * level
    return jnp.minimum(jnp.maximum(drawn, -bound), bound).astype(held_as)


def setup_inputs(seed: int = 0) -> dict:
    seeds = jax.random.split(jax.random.key(seed), 13)
    attn_queries = normal_values(seeds[0], (TOKENS, HEADS * HD), 1.0, 6.0, ((0, 8), (1, 4)), jnp.float32)
    attn_keys = normal_values(seeds[1], (TOKENS, HEADS * HD), 1.0, 6.0, ((0, 8), (1, 4)), jnp.float32)
    attn_values = normal_values(seeds[2], (TOKENS, HEADS * HD), 1.0, 6.0, ((0, 8), (1, 4)), jnp.float32)
    head_gain = jnp.clip(1.0 + 0.15 * jax.random.normal(seeds[3], (HD,), jnp.float32), 0.25, 1.75)
    out_weight = normal_values(seeds[4], (HEADS * HD, D), (HEADS * HD) ** -0.5, 0.09375, ((0, 4),))
    residual_in = normal_values(seeds[5], (TOKENS, D), 1.0, 6.0, ((0, 32),))
    norm_gain = jnp.clip(1.0 + 0.15 * jax.random.normal(seeds[6], (D,), jnp.float32), 0.25, 1.75)
    routed_experts_keys = jax.random.split(jax.random.fold_in(seeds[7], 1), TOKENS // ROWS_DEV)
    routed_experts_turns = jax.random.permutation(jax.random.fold_in(seeds[7], 3), TOKENS // ROWS_DEV)
    routed_experts = jax.vmap(lambda own, number: deal_out(jax.random.fold_in(seeds[7], 2), own, number, ROWS_DEV, EXPERTS, TOPK, CAP, 2))(routed_experts_keys, routed_experts_turns).reshape((TOKENS, TOPK))
    gate_weights = jnp.clip(0.05 + 0.95 * jax.random.uniform(seeds[8], (TOKENS, TOPK), jnp.float32) ** block_levels(seeds[8], (TOKENS, TOPK), ((0, 32),), -0.2, 0.2), 0.05, 1.0)
    expert_gate = normal_values(seeds[9], (EXPERTS, D, FF), D ** -0.5, 0.125, ((0, 32),))
    expert_up = normal_values(seeds[10], (EXPERTS, D, FF), D ** -0.5, 0.125, ((0, 32),))
    expert_down = normal_values(seeds[11], (EXPERTS, FF, D), FF ** -0.5, 0.21875, ((0, 32),))
    return dict(attn_queries=attn_queries, attn_keys=attn_keys, attn_values=attn_values, head_gain=head_gain, out_weight=out_weight, residual_in=residual_in, norm_gain=norm_gain, routed_experts=routed_experts, gate_weights=gate_weights, expert_gate=expert_gate, expert_up=expert_up, expert_down=expert_down)


block_rows = 128

def causal_linear(queries_here, keys_here, values_here, start_state, block_size):
    row_count = queries_here.shape[0]
    head_count = queries_here.shape[1]
    head_size = queries_here.shape[2]
    block_count = row_count // block_size
    lower_mask = jnp.tril(jnp.ones((block_size, block_size), jnp.float32))
    exact_mode = lax.Precision.HIGHEST

    def advance(state_now, inputs):
        query_block, key_block, value_block = inputs
        scores = jnp.einsum('thd,shd->hts', query_block, key_block, precision=exact_mode) * lower_mask
        within = jnp.einsum('hts,she->the', scores, value_block, precision=exact_mode)
        carried = jnp.einsum('thd,hde->the', query_block, state_now, precision=exact_mode)
        state_next = state_now + jnp.einsum('thd,the->hde', key_block, value_block, precision=exact_mode)
        return (state_next, within + carried)

    def blocked(tensor):
        return tensor.reshape(block_count, block_size, head_count, head_size)
    state_last, outputs = lax.scan(advance, start_state, (blocked(queries_here), blocked(keys_here), blocked(values_here)))
    return outputs.reshape(row_count, head_count, head_size)

def rms_scale(tensor, gain_row):
    return tensor * lax.rsqrt(lax.optimization_barrier(jnp.mean(tensor * tensor, axis=-1, keepdims=True)) + 1e-06) * gain_row

def expert_rows(moe_input, routed_experts, expert_gate, expert_up, expert_down):
    flat_experts = routed_experts.reshape(-1).astype(jnp.int32)
    total_rows = flat_experts.shape[0]
    sorted_order = jnp.argsort(flat_experts, stable=True).astype(jnp.int32)
    token_of = (sorted_order // TOPK).astype(jnp.int32)
    member = (flat_experts[:, None] == jnp.arange(EXPERTS, dtype=jnp.int32)[None, :]).astype(jnp.int32)
    counts = lax.optimization_barrier(jnp.sum(member, axis=0)).astype(jnp.int32)
    starts = (jnp.cumsum(counts) - counts).astype(jnp.int32)
    padded_tokens = jnp.concatenate([token_of, jnp.zeros((block_rows,), jnp.int32)])
    results = jnp.zeros((total_rows + block_rows, D), jnp.bfloat16)

    def per_expert(expert, results_now):
        first_row = starts[expert]
        turn_count = (counts[expert] + block_rows - 1) // block_rows

        def per_block(turn, results_in):
            offset = (first_row + turn * block_rows).astype(jnp.int32)
            tokens_here = lax.dynamic_slice_in_dim(padded_tokens, offset, block_rows)
            picked = moe_input[tokens_here]
            gate_part = jnp.dot(picked, expert_gate[expert], preferred_element_type=jnp.float32)
            up_part = jnp.dot(picked, expert_up[expert], preferred_element_type=jnp.float32)
            hidden_act = (jax.nn.silu(gate_part) * up_part).astype(jnp.bfloat16)
            produced = jnp.dot(hidden_act, expert_down[expert], preferred_element_type=jnp.float32).astype(jnp.bfloat16)
            return lax.dynamic_update_slice(results_in, produced, (offset, jnp.zeros((), jnp.int32)))
        return lax.fori_loop(0, turn_count, per_block, results_now)
    results = lax.fori_loop(0, EXPERTS, per_expert, results)
    inverse = jnp.argsort(sorted_order).astype(jnp.int32)
    return results[inverse]

def reference(attn_queries, attn_keys, attn_values, head_gain, out_weight, residual_in, norm_gain, routed_experts, gate_weights, expert_gate, expert_up, expert_down):
    block_size = min(512, TOKENS)
    start_state = jnp.zeros((HEADS, HD, HD), jnp.float32)
    attended = causal_linear(attn_queries.reshape(TOKENS, HEADS, HD), attn_keys.reshape(TOKENS, HEADS, HD), attn_values.reshape(TOKENS, HEADS, HD), start_state, block_size)
    head_normed = rms_scale(attended, head_gain).astype(jnp.bfloat16).reshape(TOKENS, HEADS * HD)
    attn_out = jnp.dot(head_normed, out_weight, preferred_element_type=jnp.float32).astype(jnp.bfloat16)
    mixed = residual_in.astype(jnp.float32) + attn_out.astype(jnp.float32)
    moe_input = rms_scale(mixed, norm_gain).astype(jnp.bfloat16)
    expert_y = expert_rows(moe_input, routed_experts, expert_gate, expert_up, expert_down)
    picked_rows = expert_y.reshape(TOKENS, TOPK, D)
    moe_out = lax.optimization_barrier(jnp.sum(gate_weights[:, :, None] * picked_rows.astype(jnp.float32), axis=1)).astype(jnp.bfloat16)
    return (attn_out, moe_out)
```

```python
import functools

import jax
import jax.numpy as jnp
from jax import lax
from jax.experimental import pallas as pl
from jax.experimental.pallas import tpu as pltpu
from jax.sharding import PartitionSpec as P


MESH = pl.DeviceIdType.MESH
HALVES = 2


def bit_orders(seq_size):
    bits = [1 << i for i in range(seq_size.bit_length() - 1)]
    high = bits[1:]
    return (high[::-1] + bits[:1], high + bits[:1])


def experts_kernel(
    seq_size, head_size, x_ref, w_ref, wg_hbm, wu_hbm, wd_hbm, out_ref,
    rows_all, arrived, arrived_z, act, wg, wu, wd,
    gather_send, gather_recv, sum_send, sum_recv, z_send, z_recv, load_sem,
):
    me = lax.axis_index("seq")
    mz = lax.axis_index("head")
    rows = x_ref.shape[0]
    half = x_ref.shape[1] // HALVES
    slab = rows * head_size
    ff = wg.shape[1]
    orders = bit_orders(seq_size)
    bits = [1 << i for i in range(seq_size.bit_length() - 1)]

    loads = [
        pltpu.make_async_copy(src, dst, load_sem.at[i])
        for i, (src, dst) in enumerate(((wg_hbm, wg), (wu_hbm, wu), (wd_hbm, wd)))
    ]
    for load in loads:
        load.start()

    barrier = pltpu.get_barrier_semaphore()
    for bit in bits:
        pl.semaphore_signal(barrier, inc=1, device_id=(me ^ bit, mz), device_id_type=MESH)
    for k in range(1, head_size):
        pl.semaphore_signal(barrier, inc=1, device_id=(me, mz ^ k), device_id_type=MESH)
    pl.semaphore_wait(barrier, len(bits) + head_size - 1)

    def slab_at(j):
        return pl.ds(pl.multiple_of((me ^ j) * slab, slab), slab)

    def piece_at(j, k):
        return pl.ds(pl.multiple_of((me ^ j) * slab + (mz ^ k) * rows, rows), rows)

    def own_at(k):
        return pl.ds(pl.multiple_of((mz ^ k) * rows, rows), rows)

    def remote(src, dst, send, recv, target):
        return pltpu.make_async_remote_copy(
            src_ref=src, dst_ref=dst, send_sem=send, recv_sem=recv,
            device_id=target, device_id_type=MESH,
        )

    def gather_copy(h, to_j, k, bit):
        where = rows_all.at[h, piece_at(to_j ^ bit, k)]
        return remote(
            where, where, gather_send.at[h, to_j, k], gather_recv.at[h, to_j, k], (me ^ bit, mz)
        )

    def gather_z(h, k):
        where = rows_all.at[h, piece_at(0, 0)]
        return remote(
            where, where, gather_send.at[h, 0, k], gather_recv.at[h, 0, k], (me, mz ^ k)
        )

    def last_place(order, j):
        return max([i for i, bit in enumerate(order) if bit & j], default=-1)

    for h in range(HALVES):
        rows_all[h, piece_at(0, 0), :] = x_ref[:, h * half : (h + 1) * half]
    for k in range(1, head_size):
        for h in range(HALVES):
            gather_z(h, k).start()

    def came(h, j, k):
        if j == 0 and k == 0:
            return
        if j == 0:
            gather_z(h, k).wait_recv()
        else:
            order = orders[h]
            gather_copy(h, j, k, order[last_place(order, j)]).wait_recv()

    def pass_on(h, j, k):
        came(h, j, k)
        order = orders[h]
        for bit in order[last_place(order, j) + 1 :]:
            gather_copy(h, j ^ bit, k, bit).start()

    def sends_of(h, j):
        order = orders[h]
        for k in range(head_size):
            for bit in order[last_place(order, j) + 1 :]:
                gather_copy(h, j ^ bit, k, bit).wait_send()
        if j == 0:
            for k in range(1, head_size):
                gather_z(h, k).wait_send()

    sum_orders = [order[::-1] for order in orders]

    def send_stage(h, j):
        return min([i for i, bit in enumerate(sum_orders[h]) if bit & j], default=len(bits))

    slots = []
    for h in range(HALVES):
        table = {}
        for j in range(seq_size):
            for i in range(send_stage(h, j)):
                table[(i, j)] = len(table)
        slots.append(table)

    def sum_slab(h, j):
        slot = slots[h][(0, j ^ 1)]
        return remote(
            rows_all.at[h, slab_at(j)], arrived.at[h, slot],
            sum_send.at[h, slot, 0], sum_recv.at[h, slot, 0], (me ^ 1, mz),
        )

    def sum_piece(h, j, k, i):
        bit = sum_orders[h][i]
        slot = slots[h][(i, j ^ bit)]
        return remote(
            rows_all.at[h, piece_at(j, k)], arrived.at[h, slot, own_at(k)],
            sum_send.at[h, slot, k], sum_recv.at[h, slot, k], (me ^ bit, mz),
        )

    def sum_z(h, k):
        return remote(
            rows_all.at[h, piece_at(0, k)], arrived_z.at[h, k],
            z_send.at[h, k], z_recv.at[h, k], (me, mz ^ k),
        )

    def compute(j):
        pair = pl.ds(pl.multiple_of((me ^ j) // 2 * (2 * slab), 2 * slab), 2 * slab)
        tile = 256

        @pl.loop(0, ff // tile)
        def _(f):
            columns = pl.ds(pl.multiple_of(f * tile, tile), tile)

            def product(weight):
                total = jnp.dot(
                    rows_all[0, pair, :], weight[0:half, columns],
                    preferred_element_type=jnp.float32,
                )
                return total + jnp.dot(
                    rows_all[1, pair, :], weight[half : 2 * half, columns],
                    preferred_element_type=jnp.float32,
                )

            gate = product(wg)
            act[:, columns] = (gate / (1.0 + jnp.exp(-gate)) * product(wu)).astype(act.dtype)

        for h in range(HALVES):
            sends_of(h, j)
            sends_of(h, j ^ 1)
        scale = w_ref[pair, :]
        for h in range(HALVES):

            @pl.loop(0, half // tile)
            def _(n):
                columns = pl.ds(pl.multiple_of(n * tile, tile), tile)
                source = pl.ds(pl.multiple_of(h * half + n * tile, tile), tile)
                made = jnp.dot(act[...], wd[:, source], preferred_element_type=jnp.float32)
                rows_all[h, pair, columns] = (made * scale).astype(rows_all.dtype)

        for h in range(HALVES):
            sum_slab(h, j ^ 1).start()

    def add_up(h, j, k):
        stage = send_stage(h, j)
        here = piece_at(j, k)
        total = rows_all[h, here, :].astype(jnp.float32)
        for i in range(stage):
            if i > 0:
                bit = sum_orders[h][i]
                sum_piece(h, j ^ bit, k, i).wait_recv()
            total = total + arrived[h, slots[h][(i, j)], own_at(k), :].astype(jnp.float32)
        rows_all[h, here, :] = total.astype(rows_all.dtype)

    def finish(h, j):
        sum_slab(h, j ^ 1).wait_recv()
        stage = send_stage(h, j)
        for k in reversed(range(head_size)):
            add_up(h, j, k)
            if j:
                sum_piece(h, j, k, stage).start()
            elif k:
                sum_z(h, k).start()

    evens = [0] + sorted(
        [j for j in range(2, seq_size, 2)], key=lambda j: (bin(j).count("1"), -j)
    )
    waves = {}
    for j in evens:
        waves.setdefault(bin(j).count("1"), []).append(j)
    for wave in sorted(waves)[:2]:
        for k in range(head_size):
            for j in waves[wave]:
                for h in range(HALVES):
                    pass_on(h, j, k)
    for load in loads:
        load.wait()
    for n, j in enumerate(evens):
        if bin(j).count("1") >= 2:
            for k in range(head_size):
                for h in range(HALVES):
                    pass_on(h, j, k)
        for k in range(head_size):
            for h in range(HALVES):
                came(h, j ^ 1, k)
        compute(j)
        if n >= 2:
            before = evens[n - 1]
            for h in range(HALVES):
                if send_stage(h, before) == 1:
                    finish(h, before)
    for stage in range(1, len(bits) + 1):
        for j in evens[::-1]:
            for h in range(HALVES):
                done = stage == 1 and j in evens[1:-1]
                if send_stage(h, j) == stage and not done:
                    finish(h, j)
    for h in range(HALVES):
        total = rows_all[h, piece_at(0, 0), :].astype(jnp.float32)
        for k in range(1, head_size):
            sum_z(h, k).wait_recv()
            total = total + arrived_z[h, k].astype(jnp.float32)
        out_ref[:, h * half : (h + 1) * half] = total.astype(out_ref.dtype)
    for h in range(HALVES):
        for j in range(1, seq_size):
            stage = send_stage(h, j)
            if stage == 0:
                sum_slab(h, j).wait_send()
            else:
                for k in range(head_size):
                    sum_piece(h, j, k, stage).wait_send()
        for k in range(1, head_size):
            sum_z(h, k).wait_send()


def experts_of_all(moe_input, weight_here, gate, up, down):
    seq_size, head_size = lax.axis_size("seq"), lax.axis_size("head")
    rows, width = moe_input.shape
    ff = gate.shape[1]
    tokens = rows * seq_size * head_size
    slab = rows * head_size
    half = width // HALVES
    vmem = pl.BlockSpec(memory_space=pltpu.VMEM)
    hbm = pl.BlockSpec(memory_space=pl.ANY)
    gather_sems = pltpu.SemaphoreType.DMA((HALVES, seq_size, head_size))
    return pl.pallas_call(
        functools.partial(experts_kernel, seq_size, head_size),
        out_shape=jax.ShapeDtypeStruct((rows, width), jnp.bfloat16),
        in_specs=[vmem, vmem, hbm, hbm, hbm],
        out_specs=vmem,
        scratch_shapes=[
            pltpu.VMEM((HALVES, tokens, half), jnp.bfloat16),
            pltpu.VMEM((HALVES, seq_size - 1, slab, half), jnp.bfloat16),
            pltpu.VMEM((HALVES, head_size, rows, half), jnp.bfloat16),
            pltpu.VMEM((2 * slab, ff), jnp.bfloat16),
            pltpu.VMEM((width, ff), jnp.bfloat16),
            pltpu.VMEM((width, ff), jnp.bfloat16),
            pltpu.VMEM((ff, width), jnp.bfloat16),
            gather_sems, gather_sems, gather_sems, gather_sems,
            pltpu.SemaphoreType.DMA((HALVES, head_size)),
            pltpu.SemaphoreType.DMA((HALVES, head_size)),
            pltpu.SemaphoreType.DMA((3,)),
        ],
        compiler_params=pltpu.CompilerParams(
            collective_id=1, has_side_effects=True, vmem_limit_bytes=60 * 1024 * 1024
        ),
        cost_estimate=pl.CostEstimate(
            flops=6 * tokens * width * ff, bytes_accessed=6 * width * ff, transcendentals=tokens * ff
        ),
        name="experts_of_all",
    )(moe_input, weight_here, gate, up, down)


def causal_linear(queries_here, keys_here, values_here, start_state, block_size):
    row_count = queries_here.shape[0]
    head_count = queries_here.shape[1]
    head_size = queries_here.shape[2]
    block_count = row_count // block_size
    lower_mask = jnp.tril(jnp.ones((block_size, block_size), jnp.float32))
    exact_mode = lax.Precision.HIGHEST

    def advance(state_now, inputs):
        query_block, key_block, value_block = inputs
        scores = (
            jnp.einsum("thd,shd->hts", query_block, key_block, precision=exact_mode) * lower_mask
        )
        within = jnp.einsum("hts,she->the", scores, value_block, precision=exact_mode)
        carried = jnp.einsum("thd,hde->the", query_block, state_now, precision=exact_mode)
        state_next = state_now + jnp.einsum(
            "thd,the->hde", key_block, value_block, precision=exact_mode
        )
        return (state_next, within + carried)

    def blocked(tensor):
        return tensor.reshape(block_count, block_size, head_count, head_size)

    state_last, outputs = lax.scan(
        advance, start_state, (blocked(queries_here), blocked(keys_here), blocked(values_here))
    )
    return outputs.reshape(row_count, head_count, head_size)


def rms_scale(tensor, gain_row):
    return tensor * lax.rsqrt(jnp.mean(tensor * tensor, axis=-1, keepdims=True) + 1e-06) * gain_row


def shards(
    attn_queries,
    attn_keys,
    attn_values,
    head_gain,
    out_weight,
    residual_in,
    norm_gain,
    routed_experts,
    gate_weights,
    expert_gate,
    expert_up,
    expert_down,
):
    token_count = attn_queries.shape[0]
    head_size = head_gain.shape[0]
    heads_here = attn_queries.shape[1] // head_size
    block_size = min(512, token_count)
    queries_here = attn_queries.reshape(token_count, heads_here, head_size)
    keys_here = attn_keys.reshape(token_count, heads_here, head_size)
    values_here = attn_values.reshape(token_count, heads_here, head_size)
    totals = jnp.einsum("thd,the->hde", keys_here, values_here, precision=lax.Precision.HIGHEST)

    every_total = lax.all_gather(totals.astype(jnp.bfloat16), "seq")
    earlier = jnp.arange(every_total.shape[0]) < lax.axis_index("seq")
    prefix_state = jnp.sum(
        jnp.where(earlier[:, None, None, None], every_total.astype(jnp.float32), 0.0), axis=0
    )
    attended = causal_linear(queries_here, keys_here, values_here, prefix_state, block_size)
    head_normed = (
        rms_scale(attended, head_gain)
        .astype(jnp.bfloat16)
        .reshape(token_count, heads_here * head_size)
    )
    row_share = token_count // lax.axis_size("head")
    attn_out = lax.psum_scatter(
        jnp.dot(head_normed, out_weight, preferred_element_type=jnp.float32).astype(jnp.bfloat16),
        "head",
        scatter_dimension=0,
        tiled=True,
    )
    mixed = residual_in.astype(jnp.float32) + attn_out.astype(jnp.float32)
    moe_input = rms_scale(mixed, norm_gain).astype(jnp.bfloat16)
    device = lax.axis_index("seq") * lax.axis_size("head") + lax.axis_index("head")
    expert_count = lax.axis_size("seq") * lax.axis_size("head")
    named = routed_experts[:, :, None] == jnp.arange(expert_count, dtype=jnp.int32)[None, None, :]
    weight_table = jnp.sum(jnp.where(named, gate_weights[:, :, None], 0.0), axis=1)
    every_weight = lax.all_gather(weight_table, ("seq", "head"), tiled=True)
    here = jnp.arange(expert_count, dtype=jnp.int32)[None, :] == device
    weight_here = jnp.sum(jnp.where(here, every_weight, 0.0), axis=1, keepdims=True)
    moe_out = experts_of_all(
        moe_input, weight_here, expert_gate[0], expert_up[0], expert_down[0]
    )
    return (attn_out, moe_out)


def solution(mesh):
    return jax.shard_map(
        shards,
        mesh=mesh,
        in_specs=(
            P("seq", "head"),
            P("seq", "head"),
            P("seq", "head"),
            P(),
            P("head", None),
            P(("seq", "head"), None),
            P(),
            P(("seq", "head"), None),
            P(("seq", "head"), None),
            P(("seq", "head"), None, None),
            P(("seq", "head"), None, None),
            P(("seq", "head"), None, None),
        ),
        out_specs=(P(("seq", "head"), None), P(("seq", "head"), None)),
        check_vma=False,
    )
```

```python
import functools

import jax
import jax.numpy as jnp
from jax import lax
from jax.experimental import pallas as pl
from jax.experimental.pallas import tpu as pltpu
from jax.sharding import PartitionSpec as P


MESH = pl.DeviceIdType.MESH
HALVES = 2


def bit_orders(seq_size):
    bits = [1 << i for i in range(seq_size.bit_length() - 1)]
    high = bits[1:]
    return (high[::-1] + bits[:1], high + bits[:1])


def last_place(order, j):
    return max([i for i, bit in enumerate(order) if bit & j], default=-1)


def first_place(order, j):
    return min([i for i, bit in enumerate(order) if bit & j], default=len(order))


def slot_table(order, size):
    table = {}
    for j in range(size):
        for i in range(first_place(order, j)):
            table[(i, j)] = len(table)
    return table


def remote(src, dst, send, recv, target):
    return pltpu.make_async_remote_copy(
        src_ref=src, dst_ref=dst, send_sem=send, recv_sem=recv,
        device_id=target, device_id_type=MESH,
    )


def greet(targets):
    barrier = pltpu.get_barrier_semaphore()
    for target in targets:
        pl.semaphore_signal(barrier, inc=1, device_id=target, device_id_type=MESH)
    pl.semaphore_wait(barrier, len(targets))


def attention_kernel(
    seq_size, head_size, q_ref, k_ref, v_ref, gain_ref, wo_hbm, res_ref, norm_ref, table_ref,
    attn_ref, input_ref, table_out,
    wo, totals, arrived_totals, prefix_out, prefix, attended, normed, partial, arrived, tables_z, tables,
    a_send, a_recv, b_send, b_recv, p_send, p_recv, tz_send, tz_recv, ts_send, ts_recv, load_sem,
):
    me = lax.axis_index("seq")
    mz = lax.axis_index("head")
    size = gain_ref.shape[1]
    heads = q_ref.shape[1] // size
    token_count = q_ref.shape[0]
    chunk = totals.shape[0] // seq_size
    rows = res_ref.shape[0]
    width = wo.shape[1]
    tile = partial.shape[2]
    tiles = width // tile
    order = [1 << i for i in range(head_size.bit_length() - 1)]
    slots = slot_table(order, head_size)

    load = pltpu.make_async_copy(wo_hbm, wo, load_sem)
    load.start()
    greet(
        [(me ^ j, mz) for j in range(1, seq_size)] + [(me, mz ^ k) for k in range(1, head_size)]
    )

    def table_z(k):
        return remote(
            table_ref.at[mz ^ k], tables_z.at[mz], tz_send.at[k], tz_recv.at[k], (me, mz ^ k)
        )

    for k in range(1, head_size):
        table_z(k).start()
    tables_z[mz] = table_ref[mz]

    def columns(h):
        return slice(h * size, (h + 1) * size)

    for h in range(heads):
        total = lax.dot_general(
            k_ref[:, columns(h)].astype(jnp.bfloat16), v_ref[:, columns(h)].astype(jnp.bfloat16),
            (((0,), (0,)), ((), ())), preferred_element_type=jnp.float32,
        )
        totals[columns(h), :] = total.astype(totals.dtype)

    def total_copy(j):
        source = totals.at[pl.ds(pl.multiple_of((me ^ j) * chunk, chunk), chunk)]
        return remote(source, arrived_totals.at[j], a_send.at[j], a_recv.at[j], (me ^ j, mz))

    for j in range(1, seq_size):
        total_copy(j).start()
    arrived_totals[0] = totals[pl.ds(pl.multiple_of(me * chunk, chunk), chunk), :]
    for k in range(1, head_size):
        table_z(k).wait_recv()

    def table_seq(j):
        return remote(tables_z, tables.at[j], ts_send.at[j], ts_recv.at[j], (me ^ j, mz))

    for j in range(1, seq_size):
        table_seq(j).start()
    tables[0] = tables_z[...]

    def within(h):
        scores = lax.dot_general(
            q_ref[:, columns(h)], k_ref[:, columns(h)], (((1,), (1,)), ((), ())),
            precision=lax.Precision.HIGHEST, preferred_element_type=jnp.float32,
        )
        shape = (token_count, token_count)
        later = lax.broadcasted_iota(jnp.int32, shape, 1) > lax.broadcasted_iota(jnp.int32, shape, 0)
        scores = jnp.where(later, 0.0, scores).astype(jnp.bfloat16)
        attended[:, columns(h)] = jnp.dot(
            scores, v_ref[:, columns(h)].astype(jnp.bfloat16), preferred_element_type=jnp.float32
        )

    for h in range(heads // 2):
        within(h)

    def prefix_copy(j):
        return remote(
            prefix_out.at[me ^ j], prefix.at[me], b_send.at[j], b_recv.at[j], (me ^ j, mz)
        )

    for j in range(1, seq_size):
        total_copy(j).wait_recv()
    running = jnp.zeros((chunk, size), jnp.float32)
    for a in range(seq_size):
        prefix_out[a] = running.astype(prefix_out.dtype)
        running = running + arrived_totals[me ^ a].astype(jnp.float32)
    for j in range(1, seq_size):
        prefix_copy(j).start()
    prefix[me] = prefix_out[me]
    for h in range(heads // 2, heads):
        within(h)
    for j in range(1, seq_size):
        prefix_copy(j).wait_recv()
    state = prefix[...].reshape(heads * size, size)
    for h in range(heads):
        total = attended[:, columns(h)] + jnp.dot(
            q_ref[:, columns(h)].astype(jnp.bfloat16), state[columns(h), :],
            preferred_element_type=jnp.float32,
        )
        scale = lax.rsqrt(jnp.mean(total * total, axis=-1, keepdims=True) + 1e-06)
        normed[:, columns(h)] = (total * scale * gain_ref[...]).astype(normed.dtype)

    def piece_at(k):
        return pl.ds(pl.multiple_of((mz ^ k) * rows, rows), rows)

    def piece_copy(n, k):
        stage = first_place(order, k)
        bit = order[stage]
        slot = slots[(stage, k ^ bit)]
        return remote(
            partial.at[n, piece_at(k)], arrived.at[n, slot],
            p_send.at[n, slot], p_recv.at[n, slot], (me, mz ^ bit),
        )

    load.wait()
    for n in range(tiles):

        @pl.loop(0, tile // 256)
        def _(part):
            here = pl.ds(pl.multiple_of(part * 256, 256), 256)
            source = pl.ds(pl.multiple_of(n * tile + part * 256, 256), 256)
            partial[n, :, here] = jnp.dot(
                normed[...], wo[:, source], preferred_element_type=jnp.float32
            ).astype(partial.dtype)

        for k in reversed(range(head_size)):
            if first_place(order, k) == 0:
                piece_copy(n, k).start()
    for stage in range(1, len(order) + 1):
        for n in range(tiles):
            for k in reversed(range(head_size)):
                if first_place(order, k) == stage:
                    total = partial[n, piece_at(k), :].astype(jnp.float32)
                    for i in range(stage):
                        piece_copy(n, k ^ order[i]).wait_recv()
                        total = total + arrived[n, slots[(i, k)]].astype(jnp.float32)
                    if k:
                        partial[n, piece_at(k), :] = total.astype(partial.dtype)
                        piece_copy(n, k).start()
                    else:
                        attn_ref[:, n * tile : (n + 1) * tile] = total.astype(attn_ref.dtype)
    mixed = res_ref[...].astype(jnp.float32) + attn_ref[...].astype(jnp.float32)
    scale = lax.rsqrt(jnp.mean(mixed * mixed, axis=-1, keepdims=True) + 1e-06)
    input_ref[...] = (mixed * scale * norm_ref[...]).astype(input_ref.dtype)

    for j in range(1, seq_size):
        table_seq(j).wait_recv()
    for j in range(seq_size):
        row = lax.broadcasted_iota(jnp.int32, tables.shape[1:], 1) == me
        table_out[me ^ j] = jnp.sum(jnp.where(row, tables[j], 0.0), axis=1)
    for j in range(1, seq_size):
        total_copy(j).wait_send()
        prefix_copy(j).wait_send()
        table_seq(j).wait_send()
    for k in range(1, head_size):
        table_z(k).wait_send()
        for n in range(tiles):
            piece_copy(n, k).wait_send()


def attention(q, k, v, head_gain, out_weight, residual, norm_gain, table):
    seq_size, head_size = lax.axis_size("seq"), lax.axis_size("head")
    token_count, columns = q.shape
    rows, width = residual.shape
    size = head_gain.shape[0]
    tile = 512
    lanes = table.shape[2]
    vmem = pl.BlockSpec(memory_space=pltpu.VMEM)
    dma = pltpu.SemaphoreType.DMA
    bf16, f32 = jnp.bfloat16, jnp.float32
    chunk = columns // seq_size
    return pl.pallas_call(
        functools.partial(attention_kernel, seq_size, head_size),
        out_shape=[
            jax.ShapeDtypeStruct((rows, width), bf16),
            jax.ShapeDtypeStruct((rows, width), bf16),
            jax.ShapeDtypeStruct((seq_size, head_size, lanes), f32),
        ],
        in_specs=[vmem] * 4 + [pl.BlockSpec(memory_space=pl.ANY)] + [vmem] * 3,
        out_specs=[vmem] * 3,
        scratch_shapes=[
            pltpu.VMEM(out_weight.shape, bf16),
            pltpu.VMEM((columns, size), bf16),
            pltpu.VMEM((seq_size, chunk, size), bf16),
            pltpu.VMEM((seq_size, chunk, size), bf16),
            pltpu.VMEM((seq_size, chunk, size), bf16),
            pltpu.VMEM((token_count, columns), f32),
            pltpu.VMEM((token_count, columns), bf16),
            pltpu.VMEM((width // tile, token_count, tile), bf16),
            pltpu.VMEM((width // tile, head_size - 1, rows, tile), bf16),
            pltpu.VMEM((head_size, seq_size, lanes), f32),
            pltpu.VMEM((seq_size, head_size, seq_size, lanes), f32),
            dma((seq_size,)), dma((seq_size,)), dma((seq_size,)), dma((seq_size,)),
            dma((width // tile, head_size - 1)), dma((width // tile, head_size - 1)),
            dma((head_size,)), dma((head_size,)), dma((seq_size,)), dma((seq_size,)), dma,
        ],
        compiler_params=pltpu.CompilerParams(
            collective_id=0, has_side_effects=True, vmem_limit_bytes=40 * 1024 * 1024
        ),
        cost_estimate=pl.CostEstimate(
            flops=2 * token_count * columns * (width + 4 * size), bytes_accessed=2 * columns * width,
            transcendentals=0,
        ),
        name="attention",
    )(q, k, v, head_gain[None, :], out_weight, residual, norm_gain[None, :], table)


def experts_kernel(
    seq_size, head_size, x_ref, w_ref, wg_hbm, wu_hbm, wd_hbm, out_ref,
    rows_all, arrived, arrived_z, act, wg, wu, wd,
    gather_send, gather_recv, sum_send, sum_recv, z_send, z_recv, load_sem,
):
    me = lax.axis_index("seq")
    mz = lax.axis_index("head")
    rows = x_ref.shape[0]
    half = x_ref.shape[1] // HALVES
    group = rows * seq_size
    ff = wg.shape[1]
    orders = bit_orders(seq_size)
    sum_orders = [order[::-1] for order in orders]
    slots = [slot_table(order, seq_size) for order in sum_orders]
    bits = [1 << i for i in range(seq_size.bit_length() - 1)]
    stages = len(bits)
    both = range(HALVES)

    loads = [
        pltpu.make_async_copy(src, dst, load_sem.at[i])
        for i, (src, dst) in enumerate(((wg_hbm, wg), (wu_hbm, wu), (wd_hbm, wd)))
    ]
    for load in loads:
        load.start()
    greet([(me ^ bit, mz) for bit in bits] + [(me, mz ^ k) for k in range(1, head_size)])

    def piece_at(j, k):
        place = (mz ^ k) * seq_size + (me ^ j)
        return pl.ds(pl.multiple_of(place * rows, rows), rows)

    def group_at(k):
        return pl.ds(pl.multiple_of((mz ^ k) * group, group), group)

    def gather_copy(h, j, k):
        order = orders[h]
        bit = order[last_place(order, j)]
        where = rows_all.at[h, piece_at(j ^ bit, k)]
        return remote(where, where, gather_send.at[h, j, k], gather_recv.at[h, j, k], (me ^ bit, mz))

    def gather_z(h, k):
        where = rows_all.at[h, piece_at(0, 0)]
        return remote(where, where, gather_send.at[h, 0, k], gather_recv.at[h, 0, k], (me, mz ^ k))

    def came(h, j, k):
        if j:
            gather_copy(h, j, k).wait_recv()
        elif k:
            gather_z(h, k).wait_recv()

    def pass_on(h, j, k):
        came(h, j, k)
        for bit in orders[h][last_place(orders[h], j) + 1 :]:
            gather_copy(h, j ^ bit, k).start()

    def gather_step(k, step):
        for h in both:
            for j in range(0, seq_size, 2):
                if bin(j).count("1") == step:
                    pass_on(h, j, k)

    def sum_copy(h, j, k):
        stage = first_place(sum_orders[h], j)
        bit = sum_orders[h][stage]
        slot = slots[h][(stage, j ^ bit)]
        return remote(
            rows_all.at[h, piece_at(j, k)], arrived.at[h, k, slot],
            sum_send.at[h, slot, k], sum_recv.at[h, slot, k], (me ^ bit, mz),
        )

    def sum_z(h, k):
        return remote(
            rows_all.at[h, piece_at(0, k)], arrived_z.at[h, k],
            z_send.at[h, k], z_recv.at[h, k], (me, mz ^ k),
        )

    def compute(k):
        here = group_at(k)
        tile = 256
        for h in both:
            for j in range(1, seq_size, 2):
                came(h, j, k)

        @pl.loop(0, ff // tile)
        def _(f):
            columns = pl.ds(pl.multiple_of(f * tile, tile), tile)

            def product(weight):
                total = jnp.dot(
                    rows_all[0, here, :], weight[0:half, columns],
                    preferred_element_type=jnp.float32,
                )
                return total + jnp.dot(
                    rows_all[1, here, :], weight[half : 2 * half, columns],
                    preferred_element_type=jnp.float32,
                )

            gate = product(wg)
            act[:, columns] = (gate / (1.0 + jnp.exp(-gate)) * product(wu)).astype(act.dtype)

        for h in both:
            for j in range(1, seq_size):
                gather_copy(h, j, k).wait_send()
            if k == 0:
                for other in range(1, head_size):
                    gather_z(h, other).wait_send()
        scale = w_ref[here, :]
        for h in both:

            @pl.loop(0, half // tile)
            def _(n):
                columns = pl.ds(pl.multiple_of(n * tile, tile), tile)
                source = pl.ds(pl.multiple_of(h * half + n * tile, tile), tile)
                made = jnp.dot(act[...], wd[:, source], preferred_element_type=jnp.float32)
                rows_all[h, here, columns] = (made * scale).astype(rows_all.dtype)

            for j in range(1, seq_size, 2):
                sum_copy(h, j, k).start()

    def finish(h, j, k):
        stage = first_place(sum_orders[h], j)
        here = piece_at(j, k)
        total = rows_all[h, here, :].astype(jnp.float32)
        for i in range(stage):
            sum_copy(h, j ^ sum_orders[h][i], k).wait_recv()
            total = total + arrived[h, k, slots[h][(i, j)]].astype(jnp.float32)
        rows_all[h, here, :] = total.astype(rows_all.dtype)
        if j:
            sum_copy(h, j, k).start()
        elif k:
            sum_z(h, k).start()

    def sum_step(k, stage):
        for j in reversed(range(0, seq_size, 2)):
            for h in both:
                if first_place(sum_orders[h], j) == stage:
                    finish(h, j, k)

    for h in both:
        rows_all[h, piece_at(0, 0), :] = x_ref[:, h * half : (h + 1) * half]
    groups = [0] + list(range(2, head_size)) + [1]
    for k in groups[1:]:
        for h in both:
            gather_z(h, k).start()

    for time in range(len(groups) + 2 * stages):
        for n in range(len(groups)):
            step = time - n
            if 0 <= step < stages:
                gather_step(groups[n], step)
        for n in range(len(groups)):
            step = time - n - stages
            if 1 <= step <= stages:
                sum_step(groups[n], step)
        if time == stages:
            for load in loads:
                load.wait()
        if 0 <= time - stages < len(groups):
            compute(groups[time - stages])
    for h in both:
        total = rows_all[h, piece_at(0, 0), :].astype(jnp.float32)
        for k in range(1, head_size):
            sum_z(h, k).wait_recv()
            total = total + arrived_z[h, k].astype(jnp.float32)
        out_ref[:, h * half : (h + 1) * half] = total.astype(out_ref.dtype)
    for h in both:
        for k in range(head_size):
            for j in range(1, seq_size):
                sum_copy(h, j, k).wait_send()
            if k:
                sum_z(h, k).wait_send()


def experts_of_all(moe_input, weight_here, gate, up, down):
    seq_size, head_size = lax.axis_size("seq"), lax.axis_size("head")
    rows, width = moe_input.shape
    ff = gate.shape[1]
    tokens = rows * seq_size * head_size
    group = rows * seq_size
    half = width // HALVES
    vmem = pl.BlockSpec(memory_space=pltpu.VMEM)
    hbm = pl.BlockSpec(memory_space=pl.ANY)
    gather_sems = pltpu.SemaphoreType.DMA((HALVES, seq_size, head_size))
    return pl.pallas_call(
        functools.partial(experts_kernel, seq_size, head_size),
        out_shape=jax.ShapeDtypeStruct((rows, width), jnp.bfloat16),
        in_specs=[vmem, vmem, hbm, hbm, hbm],
        out_specs=vmem,
        scratch_shapes=[
            pltpu.VMEM((HALVES, tokens, half), jnp.bfloat16),
            pltpu.VMEM((HALVES, head_size, seq_size - 1, rows, half), jnp.bfloat16),
            pltpu.VMEM((HALVES, head_size, rows, half), jnp.bfloat16),
            pltpu.VMEM((group, ff), jnp.bfloat16),
            pltpu.VMEM((width, ff), jnp.bfloat16),
            pltpu.VMEM((width, ff), jnp.bfloat16),
            pltpu.VMEM((ff, width), jnp.bfloat16),
            gather_sems, gather_sems, gather_sems, gather_sems,
            pltpu.SemaphoreType.DMA((HALVES, head_size)),
            pltpu.SemaphoreType.DMA((HALVES, head_size)),
            pltpu.SemaphoreType.DMA((3,)),
        ],
        compiler_params=pltpu.CompilerParams(
            collective_id=1, has_side_effects=True, vmem_limit_bytes=60 * 1024 * 1024
        ),
        cost_estimate=pl.CostEstimate(
            flops=6 * tokens * width * ff, bytes_accessed=6 * width * ff, transcendentals=tokens * ff
        ),
        name="experts_of_all",
    )(moe_input, weight_here, gate, up, down)


def shards(
    attn_queries,
    attn_keys,
    attn_values,
    head_gain,
    out_weight,
    residual_in,
    norm_gain,
    routed_experts,
    gate_weights,
    expert_gate,
    expert_up,
    expert_down,
):
    seq_size, head_size = lax.axis_size("seq"), lax.axis_size("head")
    expert_count = seq_size * head_size
    rows = routed_experts.shape[0]
    lanes = 128
    named = routed_experts.T[:, None, :] == jnp.arange(expert_count, dtype=jnp.int32)[None, :, None]
    table = jnp.sum(jnp.where(named, gate_weights.T[:, None, :], 0.0), axis=0)
    table = jnp.transpose(table.reshape(seq_size, head_size, rows), (1, 0, 2))
    table = jnp.pad(table, ((0, 0), (0, 0), (0, lanes - rows)))
    attn_out, moe_input, weights = attention(
        attn_queries, attn_keys, attn_values, head_gain, out_weight, residual_in, norm_gain, table
    )
    weight_here = jnp.transpose(weights[:, :, :rows], (1, 0, 2)).reshape(-1, 1)
    moe_out = experts_of_all(
        moe_input, weight_here, expert_gate[0], expert_up[0], expert_down[0]
    )
    return (attn_out, moe_out)


def solution(mesh):
    return jax.shard_map(
        shards,
        mesh=mesh,
        in_specs=(
            P("seq", "head"),
            P("seq", "head"),
            P("seq", "head"),
            P(),
            P("head", None),
            P(("seq", "head"), None),
            P(),
            P(("seq", "head"), None),
            P(("seq", "head"), None),
            P(("seq", "head"), None, None),
            P(("seq", "head"), None, None),
            P(("seq", "head"), None, None),
        ),
        out_specs=(P(("seq", "head"), None), P(("seq", "head"), None)),
        check_vma=False,
    )
```

```python
import functools

import jax
import jax.numpy as jnp
from jax import lax
from jax.experimental import pallas as pl
from jax.experimental.pallas import tpu as pltpu
from jax.sharding import PartitionSpec as P


MESH = pl.DeviceIdType.MESH
HALVES = 2


def bit_orders(seq_size):
    bits = [1 << i for i in range(seq_size.bit_length() - 1)]
    high = bits[1:]
    return (high[::-1] + bits[:1], high + bits[:1])


def last_place(order, j):
    return max([i for i, bit in enumerate(order) if bit & j], default=-1)


def first_place(order, j):
    return min([i for i, bit in enumerate(order) if bit & j], default=len(order))


def slot_table(order, size):
    table = {}
    for j in range(size):
        for i in range(first_place(order, j)):
            table[(i, j)] = len(table)
    return table


def remote(src, dst, send, recv, target):
    return pltpu.make_async_remote_copy(
        src_ref=src, dst_ref=dst, send_sem=send, recv_sem=recv,
        device_id=target, device_id_type=MESH,
    )


def layer_kernel(
    seq_size, head_size, table_hbm, q_hbm, k_hbm, v_hbm, gain_hbm, wo_hbm, res_hbm, norm_hbm,
    wg_hbm, wu_hbm, wd_hbm, attn_ref, moe_ref,
    table_ref, q_ref, k_ref, v_ref, gain_ref, wo, res_ref, norm_ref, wg, wu, wd,
    totals, arrived_totals, prefix_out, prefix, attended, normed, partial, arrived_p, tables_z, tables,
    weight_of, rows_all, arrived, arrived_z, act,
    a_send, a_recv, b_send, b_recv, p_send, p_recv, tz_send, tz_recv, ts_send, ts_recv,
    gather_send, gather_recv, sum_send, sum_recv, z_send, z_recv, load_sem,
):
    sources = (
        k_hbm, v_hbm, table_hbm, q_hbm, gain_hbm, wo_hbm, res_hbm, norm_hbm, wg_hbm, wu_hbm, wd_hbm
    )
    places = (k_ref, v_ref, table_ref, q_ref, gain_ref, wo, res_ref, norm_ref, wg, wu, wd)
    me = lax.axis_index("seq")
    mz = lax.axis_index("head")
    size = gain_ref.shape[1]
    heads = q_ref.shape[1] // size
    token_count = q_ref.shape[0]
    chunk = totals.shape[0] // seq_size
    rows = res_ref.shape[0]
    width = wo.shape[1]
    tile = partial.shape[2]
    tiles = width // tile
    order = [1 << i for i in range(head_size.bit_length() - 1)]
    head_slots = slot_table(order, head_size)

    names = ("k", "v", "table", "q", "gain", "wo", "res", "norm", "gate", "up", "down")
    loads = {
        name: pltpu.make_async_copy(src, dst, load_sem.at[i])
        for i, (name, src, dst) in enumerate(zip(names, sources, places))
    }
    for load in loads.values():
        load.start()
    barrier = pltpu.get_barrier_semaphore()
    for j in range(1, seq_size):
        pl.semaphore_signal(barrier, inc=1, device_id=(me ^ j, mz), device_id_type=MESH)
    for k in range(1, head_size):
        pl.semaphore_signal(barrier, inc=1, device_id=(me, mz ^ k), device_id_type=MESH)

    def table_z(k):
        return remote(
            table_ref.at[mz ^ k], tables_z.at[mz], tz_send.at[k], tz_recv.at[k], (me, mz ^ k)
        )

    def columns(h):
        return slice(h * size, (h + 1) * size)

    loads["k"].wait()
    loads["v"].wait()
    for h in range(heads):
        total = lax.dot_general(
            k_ref[:, columns(h)].astype(jnp.bfloat16), v_ref[:, columns(h)].astype(jnp.bfloat16),
            (((0,), (0,)), ((), ())), preferred_element_type=jnp.float32,
        )
        totals[columns(h), :] = total.astype(totals.dtype)

    pl.semaphore_wait(barrier, seq_size + head_size - 2)

    def total_copy(j):
        source = totals.at[pl.ds(pl.multiple_of((me ^ j) * chunk, chunk), chunk)]
        return remote(source, arrived_totals.at[j], a_send.at[j], a_recv.at[j], (me ^ j, mz))

    for j in range(1, seq_size):
        total_copy(j).start()
    loads["table"].wait()
    for k in range(1, head_size):
        table_z(k).start()
    tables_z[mz] = table_ref[mz]
    arrived_totals[0] = totals[pl.ds(pl.multiple_of(me * chunk, chunk), chunk), :]
    for k in range(1, head_size):
        table_z(k).wait_recv()

    def table_seq(j):
        return remote(tables_z, tables.at[j], ts_send.at[j], ts_recv.at[j], (me ^ j, mz))

    for j in range(1, seq_size):
        table_seq(j).start()
    tables[0] = tables_z[...]

    def within(h):
        scores = lax.dot_general(
            q_ref[:, columns(h)], k_ref[:, columns(h)], (((1,), (1,)), ((), ())),
            precision=lax.Precision.HIGHEST, preferred_element_type=jnp.float32,
        )
        shape = (token_count, token_count)
        later = lax.broadcasted_iota(jnp.int32, shape, 1) > lax.broadcasted_iota(jnp.int32, shape, 0)
        scores = jnp.where(later, 0.0, scores).astype(jnp.bfloat16)
        attended[:, columns(h)] = jnp.dot(
            scores, v_ref[:, columns(h)].astype(jnp.bfloat16), preferred_element_type=jnp.float32
        )

    loads["q"].wait()
    for h in range(heads // 2):
        within(h)

    def prefix_copy(j):
        return remote(
            prefix_out.at[me ^ j], prefix.at[me], b_send.at[j], b_recv.at[j], (me ^ j, mz)
        )

    for j in range(1, seq_size):
        total_copy(j).wait_recv()
    running = jnp.zeros((chunk, size), jnp.float32)
    for a in range(seq_size):
        prefix_out[a] = running.astype(prefix_out.dtype)
        running = running + arrived_totals[me ^ a].astype(jnp.float32)
    for j in range(1, seq_size):
        prefix_copy(j).start()
    prefix[me] = prefix_out[me]
    for h in range(heads // 2, heads):
        within(h)
    for j in range(1, seq_size):
        prefix_copy(j).wait_recv()
    loads["gain"].wait()
    state = prefix[...].reshape(heads * size, size)
    for h in range(heads):
        total = attended[:, columns(h)] + jnp.dot(
            q_ref[:, columns(h)].astype(jnp.bfloat16), state[columns(h), :],
            preferred_element_type=jnp.float32,
        )
        scale = lax.rsqrt(jnp.mean(total * total, axis=-1, keepdims=True) + 1e-06)
        normed[:, columns(h)] = (total * scale * gain_ref[...]).astype(normed.dtype)

    def gathered_at(j, k):
        place = (mz ^ k) * seq_size + (me ^ j)
        return pl.ds(pl.multiple_of(place * rows, rows), rows)

    def piece_at(k):
        return pl.ds(pl.multiple_of((mz ^ k) * rows, rows), rows)

    def piece_copy(n, k):
        stage = first_place(order, k)
        bit = order[stage]
        slot = head_slots[(stage, k ^ bit)]
        return remote(
            partial.at[n, piece_at(k)], arrived_p.at[n, slot],
            p_send.at[n, slot], p_recv.at[n, slot], (me, mz ^ bit),
        )

    loads["wo"].wait()
    for n in range(tiles):

        @pl.loop(0, tile // 256)
        def _(part):
            here = pl.ds(pl.multiple_of(part * 256, 256), 256)
            source = pl.ds(pl.multiple_of(n * tile + part * 256, 256), 256)
            partial[n, :, here] = jnp.dot(
                normed[...], wo[:, source], preferred_element_type=jnp.float32
            ).astype(partial.dtype)

        for k in reversed(range(head_size)):
            if first_place(order, k) == 0:
                piece_copy(n, k).start()
    for j in range(1, seq_size):
        table_seq(j).wait_recv()
    for j in range(seq_size):
        for k in range(head_size):
            turned = tables[j, mz ^ k].T
            mine = lax.broadcasted_iota(jnp.int32, turned.shape, 1) == me
            column = jnp.sum(jnp.where(mine, turned, 0.0), axis=1, keepdims=True)
            weight_of[gathered_at(j, k), :] = column[0:rows]

    for stage in range(1, len(order) + 1):
        for n in range(tiles):
            for k in reversed(range(head_size)):
                if first_place(order, k) == stage:
                    total = partial[n, piece_at(k), :].astype(jnp.float32)
                    for i in range(stage):
                        piece_copy(n, k ^ order[i]).wait_recv()
                        total = total + arrived_p[n, head_slots[(i, k)]].astype(jnp.float32)
                    if k:
                        partial[n, piece_at(k), :] = total.astype(partial.dtype)
                        piece_copy(n, k).start()
                    else:
                        attn_ref[:, n * tile : (n + 1) * tile] = total.astype(attn_ref.dtype)
    loads["res"].wait()
    loads["norm"].wait()
    mixed = res_ref[...].astype(jnp.float32) + attn_ref[...].astype(jnp.float32)
    scale = lax.rsqrt(jnp.mean(mixed * mixed, axis=-1, keepdims=True) + 1e-06)
    moe_input = (mixed * scale * norm_ref[...]).astype(rows_all.dtype)

    half = width // HALVES
    group = rows * seq_size
    ff = wg.shape[1]
    orders = bit_orders(seq_size)
    sum_orders = [order[::-1] for order in orders]
    slots = [slot_table(order, seq_size) for order in sum_orders]
    bits = [1 << i for i in range(seq_size.bit_length() - 1)]
    stages = len(bits)
    both = range(HALVES)

    def group_at(k):
        return pl.ds(pl.multiple_of((mz ^ k) * group, group), group)

    def gather_copy(h, j, k):
        order = orders[h]
        bit = order[last_place(order, j)]
        where = rows_all.at[h, gathered_at(j ^ bit, k)]
        return remote(where, where, gather_send.at[h, j, k], gather_recv.at[h, j, k], (me ^ bit, mz))

    def gather_z(h, k):
        where = rows_all.at[h, gathered_at(0, 0)]
        return remote(where, where, gather_send.at[h, 0, k], gather_recv.at[h, 0, k], (me, mz ^ k))

    def came(h, j, k):
        if j:
            gather_copy(h, j, k).wait_recv()
        elif k:
            gather_z(h, k).wait_recv()

    def pass_on(h, j, k):
        came(h, j, k)
        for bit in orders[h][last_place(orders[h], j) + 1 :]:
            gather_copy(h, j ^ bit, k).start()

    def gather_step(k, step):
        for h in both:
            for j in range(0, seq_size, 2):
                if bin(j).count("1") == step:
                    pass_on(h, j, k)

    def sum_copy(h, j, k):
        stage = first_place(sum_orders[h], j)
        bit = sum_orders[h][stage]
        slot = slots[h][(stage, j ^ bit)]
        return remote(
            rows_all.at[h, gathered_at(j, k)], arrived.at[h, k, slot],
            sum_send.at[h, slot, k], sum_recv.at[h, slot, k], (me ^ bit, mz),
        )

    def sum_z(h, k):
        return remote(
            rows_all.at[h, gathered_at(0, k)], arrived_z.at[h, k],
            z_send.at[h, k], z_recv.at[h, k], (me, mz ^ k),
        )

    def expand(k):
        here = group_at(k)
        tile = 256
        for h in both:
            for j in range(1, seq_size, 2):
                came(h, j, k)

        @pl.loop(0, ff // tile)
        def _(f):
            columns = pl.ds(pl.multiple_of(f * tile, tile), tile)

            def product(weight):
                total = jnp.dot(
                    rows_all[0, here, :], weight[0:half, columns],
                    preferred_element_type=jnp.float32,
                )
                return total + jnp.dot(
                    rows_all[1, here, :], weight[half : 2 * half, columns],
                    preferred_element_type=jnp.float32,
                )

            gate = product(wg)
            act[:, columns] = (gate / (1.0 + jnp.exp(-gate)) * product(wu)).astype(act.dtype)

    def reduce(k):
        here = group_at(k)
        tile = 256
        for h in both:
            for j in range(1, seq_size):
                gather_copy(h, j, k).wait_send()
            if k == 0:
                for other in range(1, head_size):
                    gather_z(h, other).wait_send()
        scale = weight_of[here, :]
        for h in both:

            @pl.loop(0, half // tile)
            def _(n):
                columns = pl.ds(pl.multiple_of(n * tile, tile), tile)
                source = pl.ds(pl.multiple_of(h * half + n * tile, tile), tile)
                made = jnp.dot(act[...], wd[:, source], preferred_element_type=jnp.float32)
                rows_all[h, here, columns] = (made * scale).astype(rows_all.dtype)

            for j in range(1, seq_size, 2):
                sum_copy(h, j, k).start()

    def finish(h, j, k):
        stage = first_place(sum_orders[h], j)
        here = gathered_at(j, k)
        total = rows_all[h, here, :].astype(jnp.float32)
        for i in range(stage):
            sum_copy(h, j ^ sum_orders[h][i], k).wait_recv()
            total = total + arrived[h, k, slots[h][(i, j)]].astype(jnp.float32)
        rows_all[h, here, :] = total.astype(rows_all.dtype)
        if j:
            sum_copy(h, j, k).start()
        elif k:
            sum_z(h, k).start()

    def sum_step(k, stage):
        for j in reversed(range(0, seq_size, 2)):
            for h in both:
                if first_place(sum_orders[h], j) == stage:
                    finish(h, j, k)

    for h in both:
        rows_all[h, gathered_at(0, 0), :] = moe_input[:, h * half : (h + 1) * half]
    for k in range(1, head_size):
        for h in both:
            gather_z(h, k).start()

    turns = list(range(1, head_size)) + [0]
    steps = {}
    for m in range(2, head_size):
        last = 2 * m - (3 if m == 2 else 4)
        for step in range(stages):
            at = last - (stages - 1 - step)
            steps.setdefault(max(at, -1), []).append((gather_step, m, step))
    for n, k in enumerate(turns):
        for step in range(1, stages + 1):
            steps.setdefault(2 * n + step, []).append((sum_step, k, step))
    for step in range(stages + 1):
        for m in (0, 1):
            if 0 <= step - m < stages:
                gather_step(m, step - m)
        if step == stages - 1:
            for act_on, k, part in steps.pop(-1, []):
                act_on(k, part)
    for name in ("gate", "up", "down"):
        loads[name].wait()
    for n, k in enumerate(turns):
        expand(k)
        for act_on, other, part in steps.pop(2 * n, []):
            act_on(other, part)
        reduce(k)
        for act_on, other, part in steps.pop(2 * n + 1, []):
            act_on(other, part)
    for place in sorted(steps):
        for act_on, other, part in steps[place]:
            act_on(other, part)
    for h in both:
        total = rows_all[h, gathered_at(0, 0), :].astype(jnp.float32)
        for k in range(1, head_size):
            sum_z(h, k).wait_recv()
            total = total + arrived_z[h, k].astype(jnp.float32)
        moe_ref[:, h * half : (h + 1) * half] = total.astype(moe_ref.dtype)
    for h in both:
        for k in range(head_size):
            for j in range(1, seq_size):
                sum_copy(h, j, k).wait_send()
            if k:
                sum_z(h, k).wait_send()
    for j in range(1, seq_size):
        total_copy(j).wait_send()
        prefix_copy(j).wait_send()
        table_seq(j).wait_send()
    for k in range(1, head_size):
        table_z(k).wait_send()
        for n in range(tiles):
            piece_copy(n, k).wait_send()


def layer(table, q, k, v, head_gain, out_weight, residual, norm_gain, gate, up, down):
    seq_size, head_size = lax.axis_size("seq"), lax.axis_size("head")
    token_count, columns = q.shape
    rows, width = residual.shape
    size = head_gain.shape[0]
    ff = gate.shape[1]
    tile = 512
    tiles = width // tile
    lanes = table.shape[2]
    half = width // HALVES
    group = rows * seq_size
    tokens = group * head_size
    chunk = columns // seq_size
    dma = pltpu.SemaphoreType.DMA
    bf16, f32 = jnp.bfloat16, jnp.float32
    operands = (
        table, q, k, v, head_gain[None, :], out_weight, residual, norm_gain[None, :], gate, up, down
    )
    seq_sems = dma((seq_size,))
    head_sems = dma((head_size,))
    part_sems = dma((tiles, head_size - 1))
    piece_sems = dma((HALVES, seq_size, head_size))
    z_sems = dma((HALVES, head_size))
    return pl.pallas_call(
        functools.partial(layer_kernel, seq_size, head_size),
        out_shape=[jax.ShapeDtypeStruct((rows, width), bf16)] * 2,
        in_specs=[pl.BlockSpec(memory_space=pl.ANY)] * len(operands),
        out_specs=[pl.BlockSpec(memory_space=pltpu.VMEM)] * 2,
        scratch_shapes=[pltpu.VMEM(o.shape, o.dtype) for o in operands]
        + [
            pltpu.VMEM((columns, size), bf16),
            pltpu.VMEM((seq_size, chunk, size), bf16),
            pltpu.VMEM((seq_size, chunk, size), bf16),
            pltpu.VMEM((seq_size, chunk, size), bf16),
            pltpu.VMEM((token_count, columns), f32),
            pltpu.VMEM((token_count, columns), bf16),
            pltpu.VMEM((tiles, token_count, tile), bf16),
            pltpu.VMEM((tiles, head_size - 1, rows, tile), bf16),
            pltpu.VMEM((head_size, seq_size, lanes), f32),
            pltpu.VMEM((seq_size, head_size, seq_size, lanes), f32),
            pltpu.VMEM((tokens, 1), f32),
            pltpu.VMEM((HALVES, tokens, half), bf16),
            pltpu.VMEM((HALVES, head_size, seq_size - 1, rows, half), bf16),
            pltpu.VMEM((HALVES, head_size, rows, half), bf16),
            pltpu.VMEM((group, ff), bf16),
            seq_sems, seq_sems, seq_sems, seq_sems, part_sems, part_sems,
            head_sems, head_sems, seq_sems, seq_sems,
            piece_sems, piece_sems, piece_sems, piece_sems, z_sems, z_sems,
            dma((len(operands),)),
        ],
        compiler_params=pltpu.CompilerParams(
            collective_id=0, has_side_effects=True, vmem_limit_bytes=60 * 1024 * 1024
        ),
        cost_estimate=pl.CostEstimate(
            flops=6 * tokens * width * ff, bytes_accessed=6 * width * ff, transcendentals=tokens * ff
        ),
        name="layer",
    )(*operands)


def shards(
    attn_queries,
    attn_keys,
    attn_values,
    head_gain,
    out_weight,
    residual_in,
    norm_gain,
    routed_experts,
    gate_weights,
    expert_gate,
    expert_up,
    expert_down,
):
    seq_size, head_size = lax.axis_size("seq"), lax.axis_size("head")
    expert_count = seq_size * head_size
    rows = routed_experts.shape[0]
    lanes = 128
    named = routed_experts.T[:, None, :] == jnp.arange(expert_count, dtype=jnp.int32)[None, :, None]
    table = jnp.sum(jnp.where(named, gate_weights.T[:, None, :], 0.0), axis=0)
    table = jnp.transpose(table.reshape(seq_size, head_size, rows), (1, 0, 2))
    table = jnp.pad(table, ((0, 0), (0, 0), (0, lanes - rows)))
    attn_out, moe_out = layer(
        table, attn_queries, attn_keys, attn_values, head_gain, out_weight, residual_in, norm_gain,
        expert_gate[0], expert_up[0], expert_down[0],
    )
    return (attn_out, moe_out)


def solution(mesh):
    return jax.shard_map(
        shards,
        mesh=mesh,
        in_specs=(
            P("seq", "head"),
            P("seq", "head"),
            P("seq", "head"),
            P(),
            P("head", None),
            P(("seq", "head"), None),
            P(),
            P(("seq", "head"), None),
            P(("seq", "head"), None),
            P(("seq", "head"), None, None),
            P(("seq", "head"), None, None),
            P(("seq", "head"), None, None),
        ),
        out_specs=(P(("seq", "head"), None), P(("seq", "head"), None)),
        check_vma=False,
    )
```

```python
import functools

import jax
import jax.numpy as jnp
from jax import lax
from jax.experimental import pallas as pl
from jax.experimental.pallas import tpu as pltpu
from jax.sharding import PartitionSpec as P


MESH = pl.DeviceIdType.MESH
HALVES = 2


def bit_orders(seq_size):
    bits = [1 << i for i in range(seq_size.bit_length() - 1)]
    high = bits[1:]
    return (high[::-1] + bits[:1], high + bits[:1])


def last_place(order, j):
    return max([i for i, bit in enumerate(order) if bit & j], default=-1)


def first_place(order, j):
    return min([i for i, bit in enumerate(order) if bit & j], default=len(order))


def slot_table(order, size):
    table = {}
    for j in range(size):
        for i in range(first_place(order, j)):
            table[(i, j)] = len(table)
    return table


def remote(src, dst, send, recv, target):
    return pltpu.make_async_remote_copy(
        src_ref=src, dst_ref=dst, send_sem=send, recv_sem=recv,
        device_id=target, device_id_type=MESH,
    )


def layer_kernel(
    seq_size, head_size, table_hbm, q_hbm, k_hbm, v_hbm, gain_hbm, wo_hbm, res_hbm, norm_hbm,
    wg_hbm, wu_hbm, wd_hbm, attn_ref, moe_ref,
    table_ref, q_ref, k_ref, v_ref, gain_ref, wo, res_ref, norm_ref, wg, wu, wd,
    totals, arrived_totals, prefix_out, prefix, attended, normed, partial, arrived_p, tables_z, tables,
    weight_of, rows_all, arrived, arrived_z, act,
    a_send, a_recv, b_send, b_recv, p_send, p_recv, tz_send, tz_recv, ts_send, ts_recv,
    gather_send, gather_recv, sum_send, sum_recv, z_send, z_recv, load_sem,
):
    sources = (
        k_hbm, v_hbm, table_hbm, q_hbm, gain_hbm, wo_hbm, res_hbm, norm_hbm, wg_hbm, wu_hbm, wd_hbm
    )
    places = (k_ref, v_ref, table_ref, q_ref, gain_ref, wo, res_ref, norm_ref, wg, wu, wd)
    me = lax.axis_index("seq")
    mz = lax.axis_index("head")
    size = gain_ref.shape[1]
    heads = q_ref.shape[1] // size
    token_count = q_ref.shape[0]
    chunk = totals.shape[0] // seq_size
    rows = res_ref.shape[0]
    part = rows // HALVES
    width = wo.shape[1]
    tile = partial.shape[2]
    tiles = width // tile
    order = [1 << i for i in range(head_size.bit_length() - 1)]
    head_slots = slot_table(order, head_size)

    names = ("k", "v", "table", "q", "gain", "wo", "res", "norm", "gate", "up", "down")
    loads = {
        name: pltpu.make_async_copy(src, dst, load_sem.at[i])
        for i, (name, src, dst) in enumerate(zip(names, sources, places))
    }
    for load in loads.values():
        load.start()
    barrier = pltpu.get_barrier_semaphore()
    for j in range(1, seq_size):
        pl.semaphore_signal(barrier, inc=1, device_id=(me ^ j, mz), device_id_type=MESH)
    for k in range(1, head_size):
        pl.semaphore_signal(barrier, inc=1, device_id=(me, mz ^ k), device_id_type=MESH)

    def table_z(k):
        return remote(
            table_ref.at[mz ^ k], tables_z.at[mz], tz_send.at[k], tz_recv.at[k], (me, mz ^ k)
        )

    def columns(h):
        return slice(h * size, (h + 1) * size)

    loads["k"].wait()
    loads["v"].wait()
    for h in range(heads):
        total = lax.dot_general(
            k_ref[:, columns(h)].astype(jnp.bfloat16), v_ref[:, columns(h)].astype(jnp.bfloat16),
            (((0,), (0,)), ((), ())), preferred_element_type=jnp.float32,
        )
        totals[columns(h), :] = total.astype(totals.dtype)

    pl.semaphore_wait(barrier, seq_size + head_size - 2)

    def total_copy(j):
        source = totals.at[pl.ds(pl.multiple_of((me ^ j) * chunk, chunk), chunk)]
        return remote(source, arrived_totals.at[j], a_send.at[j], a_recv.at[j], (me ^ j, mz))

    for j in range(1, seq_size):
        total_copy(j).start()
    loads["table"].wait()
    for k in range(1, head_size):
        table_z(k).start()
    tables_z[mz] = table_ref[mz]
    arrived_totals[0] = totals[pl.ds(pl.multiple_of(me * chunk, chunk), chunk), :]
    for k in range(1, head_size):
        table_z(k).wait_recv()

    def table_seq(j):
        return remote(tables_z, tables.at[j], ts_send.at[j], ts_recv.at[j], (me ^ j, mz))

    for j in range(1, seq_size):
        table_seq(j).start()
    tables[0] = tables_z[...]

    def within(h):
        scores = lax.dot_general(
            q_ref[:, columns(h)], k_ref[:, columns(h)], (((1,), (1,)), ((), ())),
            precision=lax.Precision.HIGHEST, preferred_element_type=jnp.float32,
        )
        shape = (token_count, token_count)
        later = lax.broadcasted_iota(jnp.int32, shape, 1) > lax.broadcasted_iota(jnp.int32, shape, 0)
        scores = jnp.where(later, 0.0, scores).astype(jnp.bfloat16)
        attended[:, columns(h)] = jnp.dot(
            scores, v_ref[:, columns(h)].astype(jnp.bfloat16), preferred_element_type=jnp.float32
        )

    loads["q"].wait()
    for h in range(heads // 2):
        within(h)

    def prefix_copy(j):
        return remote(
            prefix_out.at[me ^ j], prefix.at[me], b_send.at[j], b_recv.at[j], (me ^ j, mz)
        )

    for j in range(1, seq_size):
        total_copy(j).wait_recv()
    running = jnp.zeros((chunk, size), jnp.float32)
    for a in range(seq_size):
        prefix_out[a] = running.astype(prefix_out.dtype)
        running = running + arrived_totals[me ^ a].astype(jnp.float32)
    for j in range(1, seq_size):
        prefix_copy(j).start()
    prefix[me] = prefix_out[me]
    for h in range(heads // 2, heads):
        within(h)
    for j in range(1, seq_size):
        prefix_copy(j).wait_recv()
    loads["gain"].wait()
    state = prefix[...].reshape(heads * size, size)
    for h in range(heads):
        total = attended[:, columns(h)] + jnp.dot(
            q_ref[:, columns(h)].astype(jnp.bfloat16), state[columns(h), :],
            preferred_element_type=jnp.float32,
        )
        scale = lax.rsqrt(jnp.mean(total * total, axis=-1, keepdims=True) + 1e-06)
        normed[:, columns(h)] = (total * scale * gain_ref[...]).astype(normed.dtype)

    def gathered_at(j, k):
        place = (mz ^ k) * seq_size + (me ^ j)
        return pl.ds(pl.multiple_of(place * part, part), part)

    def piece_at(h, k):
        return pl.ds(pl.multiple_of((mz ^ k) * rows + h * part, part), part)

    def piece_copy(h, n, k):
        stage = first_place(order, k)
        bit = order[stage]
        slot = head_slots[(stage, k ^ bit)]
        return remote(
            partial.at[n, piece_at(h, k)], arrived_p.at[h, n, slot],
            p_send.at[h, n, slot], p_recv.at[h, n, slot], (me, mz ^ bit),
        )

    loads["wo"].wait()
    for n in range(tiles):

        @pl.loop(0, tile // 256)
        def _(strip):
            here = pl.ds(pl.multiple_of(strip * 256, 256), 256)
            source = pl.ds(pl.multiple_of(n * tile + strip * 256, 256), 256)
            partial[n, :, here] = jnp.dot(
                normed[...], wo[:, source], preferred_element_type=jnp.float32
            ).astype(partial.dtype)

        for k in reversed(range(head_size)):
            if first_place(order, k) == 0:
                piece_copy(0, n, k).start()
    for n in range(tiles):
        for k in reversed(range(head_size)):
            if first_place(order, k) == 0:
                piece_copy(1, n, k).start()
    for j in range(1, seq_size):
        table_seq(j).wait_recv()
    for j in range(seq_size):
        for k in range(head_size):
            turned = tables[j, mz ^ k].T
            mine = lax.broadcasted_iota(jnp.int32, turned.shape, 1) == me
            column = jnp.sum(jnp.where(mine, turned, 0.0), axis=1, keepdims=True)
            for h in range(HALVES):
                weight_of[h, gathered_at(j, k), :] = column[h * part : (h + 1) * part]

    def normed_input(h):
        here = slice(h * part, (h + 1) * part)
        for stage in range(1, len(order) + 1):
            for n in range(tiles):
                for k in reversed(range(head_size)):
                    if first_place(order, k) != stage:
                        continue
                    total = partial[n, piece_at(h, k), :].astype(jnp.float32)
                    for i in range(stage):
                        piece_copy(h, n, k ^ order[i]).wait_recv()
                        total = total + arrived_p[h, n, head_slots[(i, k)]].astype(jnp.float32)
                    if k:
                        partial[n, piece_at(h, k), :] = total.astype(partial.dtype)
                        piece_copy(h, n, k).start()
                    else:
                        attn_ref[here, n * tile : (n + 1) * tile] = total.astype(attn_ref.dtype)
        mixed = res_ref[here, :].astype(jnp.float32) + attn_ref[here, :].astype(jnp.float32)
        scale = lax.rsqrt(jnp.mean(mixed * mixed, axis=-1, keepdims=True) + 1e-06)
        rows_all[h, gathered_at(0, 0), :] = (mixed * scale * norm_ref[...]).astype(rows_all.dtype)

    group = part * seq_size
    ff = wg.shape[1]
    orders = bit_orders(seq_size)
    sum_orders = [order[::-1] for order in orders]
    slots = [slot_table(order, seq_size) for order in sum_orders]
    bits = [1 << i for i in range(seq_size.bit_length() - 1)]
    stages = len(bits)
    both = range(HALVES)

    def group_at(k):
        return pl.ds(pl.multiple_of((mz ^ k) * group, group), group)

    def gather_copy(h, j, k):
        order = orders[h]
        bit = order[last_place(order, j)]
        where = rows_all.at[h, gathered_at(j ^ bit, k)]
        return remote(where, where, gather_send.at[h, j, k], gather_recv.at[h, j, k], (me ^ bit, mz))

    def gather_z(h, k):
        where = rows_all.at[h, gathered_at(0, 0)]
        return remote(where, where, gather_send.at[h, 0, k], gather_recv.at[h, 0, k], (me, mz ^ k))

    def came(h, j, k):
        if j:
            gather_copy(h, j, k).wait_recv()
        elif k:
            gather_z(h, k).wait_recv()

    def pass_on(h, j, k):
        came(h, j, k)
        for bit in orders[h][last_place(orders[h], j) + 1 :]:
            gather_copy(h, j ^ bit, k).start()

    def gather_step(h, k, step):
        for j in range(0, seq_size, 2):
            if bin(j).count("1") == step:
                pass_on(h, j, k)

    def sum_copy(h, j, k):
        stage = first_place(sum_orders[h], j)
        bit = sum_orders[h][stage]
        slot = slots[h][(stage, j ^ bit)]
        return remote(
            rows_all.at[h, gathered_at(j, k)], arrived.at[h, k, slot],
            sum_send.at[h, slot, k], sum_recv.at[h, slot, k], (me ^ bit, mz),
        )

    def sum_z(h, k):
        return remote(
            rows_all.at[h, gathered_at(0, k)], arrived_z.at[h, k],
            z_send.at[h, k], z_recv.at[h, k], (me, mz ^ k),
        )

    def expand(h, k):
        here = group_at(k)
        tile = 256
        for j in range(1, seq_size, 2):
            came(h, j, k)

        @pl.loop(0, ff // tile)
        def _(f):
            columns = pl.ds(pl.multiple_of(f * tile, tile), tile)
            gate = jnp.dot(rows_all[h, here, :], wg[:, columns], preferred_element_type=jnp.float32)
            up = jnp.dot(rows_all[h, here, :], wu[:, columns], preferred_element_type=jnp.float32)
            act[:, columns] = (gate / (1.0 + jnp.exp(-gate)) * up).astype(act.dtype)

    def reduce(h, k):
        here = group_at(k)
        tile = 512
        for j in range(1, seq_size):
            gather_copy(h, j, k).wait_send()
        if k == 0:
            for other in range(1, head_size):
                gather_z(h, other).wait_send()

        @pl.loop(0, width // tile)
        def _(n):
            columns = pl.ds(pl.multiple_of(n * tile, tile), tile)
            made = jnp.dot(act[...], wd[:, columns], preferred_element_type=jnp.float32)
            rows_all[h, here, columns] = (made * weight_of[h, here, :]).astype(rows_all.dtype)

        for j in range(1, seq_size, 2):
            sum_copy(h, j, k).start()

    def finish(h, j, k):
        stage = first_place(sum_orders[h], j)
        here = gathered_at(j, k)
        total = rows_all[h, here, :].astype(jnp.float32)
        for i in range(stage):
            sum_copy(h, j ^ sum_orders[h][i], k).wait_recv()
            total = total + arrived[h, k, slots[h][(i, j)]].astype(jnp.float32)
        rows_all[h, here, :] = total.astype(rows_all.dtype)
        if j:
            sum_copy(h, j, k).start()
        elif k:
            sum_z(h, k).start()

    def sum_step(h, k, stage):
        for j in reversed(range(0, seq_size, 2)):
            if first_place(sum_orders[h], j) == stage:
                finish(h, j, k)

    for name in ("res", "norm"):
        loads[name].wait()
    for h in both:
        normed_input(h)
        for k in range(1, head_size):
            gather_z(h, k).start()
        gather_step(h, 0, 0)

    later = [(h, k) for k in range(1, head_size) for h in both]
    turns = [(0, 0)] + later + [(1, 0)]
    steps = {}
    for step in range(1, stages):
        steps.setdefault(step - 1, []).append((gather_step, 1, 0, step))
    for m, (h, k) in enumerate(later, 2):
        last = max(2 * m - 4, 1)
        for step in range(stages):
            at = max(last - (stages - 1 - step), -1)
            steps.setdefault(at, []).append((gather_step, h, k, step))
    for n, (h, k) in enumerate(turns):
        for step in range(1, stages + 1):
            steps.setdefault(2 * n + 1 + step, []).append((sum_step, h, k, step))

    def run(place):
        for act_on, h, k, step in steps.pop(place, []):
            act_on(h, k, step)

    for step in range(1, stages):
        gather_step(0, 0, step)
    run(-1)
    for name in ("gate", "up", "down"):
        loads[name].wait()
    for n, (h, k) in enumerate(turns):
        expand(h, k)
        run(2 * n)
        reduce(h, k)
        run(2 * n + 1)
    for place in sorted(steps):
        run(place)
    for h in both:
        total = rows_all[h, gathered_at(0, 0), :].astype(jnp.float32)
        for k in range(1, head_size):
            sum_z(h, k).wait_recv()
            total = total + arrived_z[h, k].astype(jnp.float32)
        moe_ref[h * part : (h + 1) * part, :] = total.astype(moe_ref.dtype)
    for h in both:
        for k in range(head_size):
            for j in range(1, seq_size):
                sum_copy(h, j, k).wait_send()
            if k:
                sum_z(h, k).wait_send()
    for j in range(1, seq_size):
        total_copy(j).wait_send()
        prefix_copy(j).wait_send()
        table_seq(j).wait_send()
    for k in range(1, head_size):
        table_z(k).wait_send()
        for n in range(tiles):
            for h in both:
                piece_copy(h, n, k).wait_send()


def layer(table, q, k, v, head_gain, out_weight, residual, norm_gain, gate, up, down):
    seq_size, head_size = lax.axis_size("seq"), lax.axis_size("head")
    token_count, columns = q.shape
    rows, width = residual.shape
    size = head_gain.shape[0]
    ff = gate.shape[1]
    tile = 512
    tiles = width // tile
    lanes = table.shape[2]
    part = rows // HALVES
    group = part * seq_size
    tokens = rows * seq_size * head_size
    chunk = columns // seq_size
    dma = pltpu.SemaphoreType.DMA
    bf16, f32 = jnp.bfloat16, jnp.float32
    operands = (
        table, q, k, v, head_gain[None, :], out_weight, residual, norm_gain[None, :], gate, up, down
    )
    seq_sems = dma((seq_size,))
    head_sems = dma((head_size,))
    part_sems = dma((HALVES, tiles, head_size - 1))
    piece_sems = dma((HALVES, seq_size, head_size))
    z_sems = dma((HALVES, head_size))
    return pl.pallas_call(
        functools.partial(layer_kernel, seq_size, head_size),
        out_shape=[jax.ShapeDtypeStruct((rows, width), bf16)] * 2,
        in_specs=[pl.BlockSpec(memory_space=pl.ANY)] * len(operands),
        out_specs=[pl.BlockSpec(memory_space=pltpu.VMEM)] * 2,
        scratch_shapes=[pltpu.VMEM(o.shape, o.dtype) for o in operands]
        + [
            pltpu.VMEM((columns, size), bf16),
            pltpu.VMEM((seq_size, chunk, size), bf16),
            pltpu.VMEM((seq_size, chunk, size), bf16),
            pltpu.VMEM((seq_size, chunk, size), bf16),
            pltpu.VMEM((token_count, columns), f32),
            pltpu.VMEM((token_count, columns), bf16),
            pltpu.VMEM((tiles, token_count, tile), bf16),
            pltpu.VMEM((HALVES, tiles, head_size - 1, part, tile), bf16),
            pltpu.VMEM((head_size, seq_size, lanes), f32),
            pltpu.VMEM((seq_size, head_size, seq_size, lanes), f32),
            pltpu.VMEM((HALVES, tokens // HALVES, 1), f32),
            pltpu.VMEM((HALVES, tokens // HALVES, width), bf16),
            pltpu.VMEM((HALVES, head_size, seq_size - 1, part, width), bf16),
            pltpu.VMEM((HALVES, head_size, part, width), bf16),
            pltpu.VMEM((group, ff), bf16),
            seq_sems, seq_sems, seq_sems, seq_sems, part_sems, part_sems,
            head_sems, head_sems, seq_sems, seq_sems,
            piece_sems, piece_sems, piece_sems, piece_sems, z_sems, z_sems,
            dma((len(operands),)),
        ],
        compiler_params=pltpu.CompilerParams(
            collective_id=0, has_side_effects=True, vmem_limit_bytes=60 * 1024 * 1024
        ),
        cost_estimate=pl.CostEstimate(
            flops=6 * tokens * width * ff, bytes_accessed=6 * width * ff, transcendentals=tokens * ff
        ),
        name="layer",
    )(*operands)


def shards(
    attn_queries,
    attn_keys,
    attn_values,
    head_gain,
    out_weight,
    residual_in,
    norm_gain,
    routed_experts,
    gate_weights,
    expert_gate,
    expert_up,
    expert_down,
):
    seq_size, head_size = lax.axis_size("seq"), lax.axis_size("head")
    expert_count = seq_size * head_size
    rows = routed_experts.shape[0]
    lanes = 128
    named = routed_experts.T[:, None, :] == jnp.arange(expert_count, dtype=jnp.int32)[None, :, None]
    table = jnp.sum(jnp.where(named, gate_weights.T[:, None, :], 0.0), axis=0)
    table = jnp.transpose(table.reshape(seq_size, head_size, rows), (1, 0, 2))
    table = jnp.pad(table, ((0, 0), (0, 0), (0, lanes - rows)))
    attn_out, moe_out = layer(
        table, attn_queries, attn_keys, attn_values, head_gain, out_weight, residual_in, norm_gain,
        expert_gate[0], expert_up[0], expert_down[0],
    )
    return (attn_out, moe_out)


def solution(mesh):
    return jax.shard_map(
        shards,
        mesh=mesh,
        in_specs=(
            P("seq", "head"),
            P("seq", "head"),
            P("seq", "head"),
            P(),
            P("head", None),
            P(("seq", "head"), None),
            P(),
            P(("seq", "head"), None),
            P(("seq", "head"), None),
            P(("seq", "head"), None, None),
            P(("seq", "head"), None, None),
            P(("seq", "head"), None, None),
        ),
        out_specs=(P(("seq", "head"), None), P(("seq", "head"), None)),
        check_vma=False,
    )
```
